32 devices in a mesh: gx: 4 (over y, core), gy: 8 (over z, x).
Axes of the slice: x: 2, y: 2, z: 4, core: 2. Of those that a mesh axis runs over, the one named last changes fastest.
Arguments:
- outline: float32 [128, 512, 512], P('gx', 'gy'), may hold values from -0.7 to 0.7, as said below
- centres: float32 [128, 512, 2], P('gx', 'gy'), may hold values from -0.75 to 0.75
- velocity: float32 [128, 512, 2], P('gx', 'gy'), may hold values from -6 to 6
- mass: float32 [128, 512], P('gx', 'gy'), may hold values from 0.5 to 4
- response: float32 [128, 512, 64], P('gx', 'gy'), may hold values from -0.75 to 0.75
- pairs: int32 [4, 8, 512, 4], P('gx', 'gy'), may hold values from 0 to 2047, as said below
- pair_count: int32 [4, 8], P('gx', 'gy'), may hold values from 1 to 512, as said below
- forcing: float32 [65536, 128], P(('gx', 'gy')), may hold values from -6 to 6
- ocean_dest: int32 [65536, 1], P(('gx', 'gy')), may hold values from 0 to 31; in each aligned block of 2048 rows (0 to 2047, 2048 to 4095, ...) at most 160 rows name the same one
- ocean_floe: int32 [65536], P(('gx', 'gy')), may hold values from 0 to 2047
Outputs:
- final_velocity: float32 [128, 512, 2], P('gx', 'gy')
- final_centres: float32 [128, 512, 2], P('gx', 'gy')
The draws below stay inside these ranges and needn't reach their ends.
Inputs may be any that keep to these rules, and one draw needn't show every extreme that they name: `pairs`: each slot holds a local floe below 2048, a neighbour code below 8, and two tiles below 2; slots from pair_count on are padding. `pair_count`: some block's list is full. `ocean_dest`: the rows of one block name any one block at most 160 times. `outline`: polygon vertices lie at radii 0.3 to 0.7 around the centre, in order of angle.
All inputs are finite; a program needn't handle non-finite values.
Results may differ from the reference program's by a relative error of at most 0.0003.
Values sent between devices are 32-bit elements; how exact they have to be, the bound alone decides.
A program may use at most 128 MiB of HBM per device.

```python
import math
import jax
import jax.numpy as jnp
import numpy as np
from jax import lax

FX = 32
FY = 64
V = 256
TILE = 128
NB = 64
PMAX = 512
ROWS_DEV = 2048
STEPS = 3
NTILE = 2
F_DEV = 2048
NXF = 128
NYF = 512
BLKX = 4
BLKY = 8
CAP = 160
ROWS = 65536
N_GX = 4
N_GY = 8


def draw_outline(key, part):
    key = jax.random.fold_in(key, 11)
    first, second = jax.random.split(key)
    spread = 0.25
    angle_noise = jax.random.uniform(first, (NXF, NYF, V), jnp.float32, -1.0, 1.0)
    radius = 0.5 * (1.0 + spread * jax.random.uniform(second, (NXF, NYF, V), jnp.float32, -1.0, 1.0))
    theta = (jnp.arange(V, dtype=jnp.float32) + 0.3 * angle_noise) * (2.0 * math.pi / V)
    return jnp.concatenate([radius * jnp.cos(theta), radius * jnp.sin(theta)], axis=2)


def draw_pairs(key, part):
    key = jax.random.fold_in(key, 23)
    keys = jax.random.split(key, 4)
    shape = (BLKX, BLKY, PMAX, 1)
    local = jax.random.randint(keys[0], shape, 0, F_DEV)
    code = jax.random.randint(keys[1], shape, 0, 8)
    tile_own = jax.random.randint(keys[2], shape, 0, NTILE)
    tile_other = jax.random.randint(keys[3], shape, 0, NTILE)
    return jnp.concatenate([local, code, tile_own, tile_other], axis=3).astype(jnp.int32)


def draw_pair_count(key, part):
    key = jax.random.fold_in(key, 37)
    first, second = jax.random.split(key)
    counts = jax.random.randint(first, (BLKX, BLKY), max(1, PMAX // 8), PMAX // 2 + 1)
    chosen = jax.random.randint(second, (), 0, BLKX * BLKY)
    number = jnp.arange(BLKX * BLKY, dtype=jnp.int32).reshape(BLKX, BLKY)
    return jnp.where(number == chosen, PMAX, counts).astype(jnp.int32)


def touch_ends(entries, rng, smallest, high):
    place = [jax.random.randint(jax.random.fold_in(rng, axis), (), 0, length) for axis, length in enumerate(entries.shape)]
    longest = entries.shape.index(max(entries.shape))
    beside = place[:longest] + [(place[longest] + 1) % entries.shape[longest]] + place[longest + 1:]
    return entries.at[tuple(place)].set(smallest).at[tuple(beside)].set(high)


def block_scale(key, shape, cuts, smallest, top_value):
    def one(dim, parts):
        draws = jax.random.uniform(jax.random.fold_in(jax.random.fold_in(key, 6), dim), (parts,), jnp.float32, smallest / len(cuts), top_value / len(cuts))
        return jnp.repeat(jnp.exp(draws), shape[dim] // parts).reshape((-1,) + (1,) * (len(shape) - dim - 1))

    level = one(*cuts[0])
    for cut in cuts[1:]:
        level = level * one(*cut)
    return level


def shared_out(key, own, number, rows, count, top, most, slope):
    sequence = jax.random.permutation(key, count)
    heavy_load, usual = portions_of(count, rows * top, most, slope, True), portions_of(count, rows * top, most, slope, False)
    places = jnp.arange(count)

    def named(lengths, turn):
        used = int((lengths > 0).sum())
        fixed = max(1, used // 4)
        shifted = fixed + (places - fixed + turn * (used - fixed)) % max(1, count - fixed)
        return jnp.zeros((count,), jnp.int32).at[sequence[jnp.where(places < fixed, places, shifted)]].set(jnp.asarray(lengths, jnp.int32))

    lengths = jnp.where(number % 4 == 0, named(heavy_load, number // 4), named(usual, number - number // 4 - 1))
    mixed = jax.random.permutation(jax.random.fold_in(own, 3), count)
    giver, sink = mixed[0:count // 2 * 2:2], mixed[1:count // 2 * 2:2]
    slack = jnp.minimum(lengths[giver] - 1, most - lengths[sink]) // 2
    slack = jnp.where((giver == sequence[0]) | (sink == sequence[0]) | (lengths[sink] == 0), 0, jnp.maximum(slack, 0))
    shifted = jax.random.randint(jax.random.fold_in(own, 4), (count // 2,), 0, 1 << 20) % (slack + 1)
    lengths = lengths.at[giver].add(-shifted).at[sink].add(shifted)
    members = jnp.searchsorted(jnp.cumsum(lengths), jnp.arange(rows * top), side="right").astype(jnp.int32)
    grid = members.reshape(top, rows).T
    grid = grid[jax.random.permutation(jax.random.fold_in(own, 1), rows)]
    turn = jax.random.randint(jax.random.fold_in(own, 2), (rows, 1), 0, top)
    return jnp.take_along_axis(grid, (jnp.arange(top)[None, :] + turn) % top, axis=1)


def portions_of(number_of, total, reach, slope, full):
    loads = [(1 << 20) // math.isqrt(rank ** slope) + 1 for rank in range(1, number_of + 1)]
    largest = reach if full else min(reach, max(-(-total // number_of), total * loads[0] // sum(loads)))
    least = 1 if total - largest >= number_of - 1 else 0
    given, spare = [largest] + [least] * (number_of - 1), total - largest - least * (number_of - 1)
    while spare > 0:
        candidates = [i for i in range(1, number_of) if given[i] < largest] or [i for i in range(1, number_of) if given[i] < reach]
        pool, remaining = sum([loads[i] for i in candidates]), spare
        for i in candidates:
            more = min(reach - given[i], max(1, remaining * loads[i] // pool), spare)
            given[i] = given[i] + more
            spare = spare - more
    return np.array(given)


def normal_values(stream_key, dims, scale, reach, shards=(), kind=jnp.bfloat16):
    loudness = block_scale(stream_key, dims, shards, -0.22, 0.18) if shards else 1.0
    array = jax.random.normal(stream_key, dims, jnp.float32) * scale * loudness
    return jnp.minimum(jnp.maximum(array, -reach), reach).astype(kind)


def setup_inputs(seed: int = 0) -> dict:
    seeds = jax.random.split(jax.random.key(seed), 11)
    outline = draw_outline(jax.random.fold_in(seeds[10], 71), 0)
    centres = normal_values(seeds[1], (NXF, NYF, 2), 0.05, 0.75, ((0, 4), (1, 8)), jnp.float32)
    velocity = normal_values(seeds[2], (NXF, NYF, 2), 0.5, 6.0, ((0, 4), (1, 8)), jnp.float32)
    mass = jnp.clip(jnp.exp(math.log(4.0) - 2.0794415 * jax.random.uniform(seeds[3], (NXF, NYF), jnp.float32) ** block_scale(seeds[3], (NXF, NYF), ((0, 4), (1, 8)), -0.2, 0.2)), 0.5, 4.0)
    response = normal_values(seeds[4], (NXF, NYF, NB), NB ** -0.5, 0.75, ((0, 4), (1, 8)), jnp.float32)
    pairs = draw_pairs(jax.random.fold_in(seeds[10], 71), 0)
    pair_count = draw_pair_count(jax.random.fold_in(seeds[10], 71), 0)
    forcing = normal_values(seeds[7], (ROWS, 2 * NB), 1.0, 6.0, ((0, 32),), jnp.float32)
    ocean_dest_keys = jax.random.split(jax.random.fold_in(seeds[8], 1), ROWS // ROWS_DEV)
    ocean_dest_turns = jax.random.permutation(jax.random.fold_in(seeds[8], 3), ROWS // ROWS_DEV)
    ocean_dest = jax.vmap(lambda own, number: shared_out(jax.random.fold_in(seeds[8], 2), own, number, ROWS_DEV, N_GX * N_GY, 1, CAP, 2))(ocean_dest_keys, ocean_dest_turns).reshape((ROWS, 1))
    ocean_floe = touch_ends(jax.random.randint(seeds[9], (ROWS,), 0, F_DEV), jax.random.fold_in(seeds[9], 1), 0, F_DEV - 1).astype(jnp.int32)
    return dict(outline=outline, centres=centres, velocity=velocity, mass=mass, response=response, pairs=pairs, pair_count=pair_count, forcing=forcing, ocean_dest=ocean_dest, ocean_floe=ocean_floe)


DIRX = (-1, -1, -1, 0, 0, 1, 1, 1)
DIRY = (-1, 0, 1, -1, 1, -1, 0, 1)
KAPPA = 1.0
INV_WIDTH = 100.0
DT = 0.1
DRAG = 0.5


def tile_force(own, other, step_x, step_y):
    diff_x = (own[:, 0, :, None] - other[:, 0, None, :]) - step_x[:, None, None]
    diff_y = (own[:, 1, :, None] - other[:, 1, None, :]) - step_y[:, None, None]
    weight = jnp.exp(-(diff_x * diff_x + diff_y * diff_y) * INV_WIDTH)
    return KAPPA * jnp.stack([jnp.sum(weight * diff_x, axis=(1, 2)), jnp.sum(weight * diff_y, axis=(1, 2))], axis=1)


def contact_forces(positions, pairs, pair_count):
    width = NYF + 2
    flat = jnp.pad(positions, ((1, 1), (1, 1), (0, 0))).reshape(-1, 2, NTILE, TILE)
    blk_x = jnp.arange(BLKX, dtype=jnp.int32)[:, None, None]
    blk_y = jnp.arange(BLKY, dtype=jnp.int32)[None, :, None]
    local = pairs[..., 0]
    code = pairs[..., 1]
    step_x = jnp.asarray(DIRX, dtype=jnp.int32)[code]
    step_y = jnp.asarray(DIRY, dtype=jnp.int32)[code]
    row = blk_x * FX + local // FY
    col = blk_y * FY + local % FY
    prow = row + step_x
    pcol = col + step_y
    slot = jnp.arange(PMAX, dtype=jnp.int32)[None, None, :]
    valid = (slot < pair_count[..., None]) & (prow >= 0) & (prow < NXF) & (pcol >= 0) & (pcol < NYF)
    own_idx = ((row + 1) * width + col + 1).reshape(-1, PMAX)
    other_idx = ((prow + 1) * width + pcol + 1).reshape(-1, PMAX)

    def block(items):
        oi, ot, pi, pt, sx, sy, ok = items
        own = flat[oi, :, ot, :]
        other = flat[pi, :, pt, :]
        return tile_force(own, other, sx.astype(jnp.float32), sy.astype(jnp.float32)) * ok.astype(jnp.float32)[:, None]

    forces = lax.map(block, (own_idx, pairs[..., 2].reshape(-1, PMAX), other_idx, pairs[..., 3].reshape(-1, PMAX),
                             step_x.reshape(-1, PMAX), step_y.reshape(-1, PMAX), valid.reshape(-1, PMAX)))
    forces = forces.reshape(-1, 2)
    accum = jnp.zeros(((NXF + 2) * width, 2), jnp.float32)
    accum = accum.at[own_idx.reshape(-1)].add(forces).at[other_idx.reshape(-1)].add(-forces)
    return accum.reshape(NXF + 2, width, 2)[1:-1, 1:-1]


def reference(outline, centres, velocity, mass, response, pairs, pair_count, forcing, ocean_dest, ocean_floe):
    dest = ocean_dest[:, 0]
    row = (dest // BLKY) * FX + ocean_floe // FY
    col = (dest % BLKY) * FY + ocean_floe % FY
    cell = row * NYF + col
    ocean_sum = jax.ops.segment_sum(forcing, cell, num_segments=NXF * NYF).reshape(NXF, NYF, 2, NB)
    ocean_force = jnp.einsum('xycb,xyb->xyc', ocean_sum, response, precision=lax.Precision.HIGHEST)
    shift = centres
    vel = velocity
    for step in range(STEPS):
        positions = outline + jnp.repeat(shift, V, axis=2)
        contact = contact_forces(positions, pairs, pair_count)
        vel = vel + DT * ((contact + ocean_force) - DRAG * vel) / mass[..., None]
        shift = shift + DT * vel
    return vel, shift
```

```python
import functools
import math

import jax
import jax.numpy as jnp
from jax import lax
from jax.experimental import pallas as pl
from jax.experimental.pallas import tpu as pltpu
from jax.sharding import PartitionSpec as P

MESH = pl.DeviceIdType.MESH
TILE = 128
STEPS = 3

DIRX = (-1, -1, -1, 0, 0, 1, 1, 1)
DIRY = (-1, 0, 1, -1, 1, -1, 0, 1)
INV_WIDTH = 100.0
DT = 0.1
DRAG = 0.5
SCALE = math.sqrt(INV_WIDTH * math.log2(math.e))
NT = (((1,), (1,)), ((), ()))
EXACT = lax.Precision.HIGHEST
VMEM_BYTES = 48 * 1024 * 1024


def up_to(value, step):
    return -(-value // step) * step


def split_two(value):
    high = value.astype(jnp.bfloat16)
    low = (value - high.astype(jnp.float32)).astype(jnp.bfloat16)
    return jnp.concatenate([high, low], axis=1)


def hot(match):
    return jnp.where(match, 1.0, 0.0).astype(jnp.bfloat16)


def in_vmem():
    return pl.BlockSpec(memory_space=pltpu.VMEM)


def pack_kernel(devices, cap, cols, dest_ref, floe_ref, rows_ref, out_ref, place, halves, names):
    count = dest_ref.shape[1]
    width = 256
    before = hot(
        lax.broadcasted_iota(jnp.int32, (width, width), 0)
        < lax.broadcasted_iota(jnp.int32, (width, width), 1)
    )
    owner = lax.broadcasted_iota(jnp.int32, (devices, width), 0)
    offset = jnp.zeros((devices, 1), jnp.float32)
    for start in range(0, count, width):
        dest = dest_ref[:, start : start + width]
        match = owner == dest
        earlier = jnp.dot(hot(match), before, preferred_element_type=jnp.float32) + offset
        slot = jnp.sum(jnp.where(match, earlier, 0.0), axis=0, keepdims=True)
        place[:, start : start + width] = dest * cap + slot.astype(jnp.int32)
        offset = offset + jnp.sum(jnp.where(match, 1.0, 0.0), axis=1, keepdims=True)
    halves[...] = split_two(rows_ref[...])
    floe = floe_ref[...]
    names[...] = jnp.concatenate(
        [(floe // cols).astype(jnp.float32), (floe % cols).astype(jnp.float32)]
        + [jnp.zeros((1, count), jnp.float32)] * 14,
        axis=0,
    ).astype(jnp.bfloat16)

    def one(device, carry):
        slots = lax.broadcasted_iota(jnp.int32, (cap, count), 0) + device * cap
        chosen = hot(slots == place[...])
        both = jnp.dot(chosen, halves[...], preferred_element_type=jnp.float32)
        out_ref[device, 0:cap, :] = both[:, :128] + both[:, 128:]
        name = lax.dot_general(names[...], chosen, NT, preferred_element_type=jnp.float32)
        local = name[0:1] * float(cols) + name[1:2]
        out_ref[device, cap : cap + 8, :] = jnp.zeros((8, 128), jnp.float32)
        for start in range(0, cap, 128):
            size = min(128, cap - start)
            line = cap + start // 128
            out_ref[device, line : line + 1, 0:size] = local[:, start : start + size]
        return carry

    lax.fori_loop(0, devices, one, 0)


def ocean_kernel(devices, cap, index_ref, rows_ref, response_ref, out_ref, halves):
    total = devices * cap
    block = 256

    def split(device, carry):
        start = pl.multiple_of(device * cap, 16)
        halves[pl.ds(start, cap), :] = split_two(rows_ref[device, 0:cap, :])
        return carry

    lax.fori_loop(0, devices, split, 0)
    lane = lax.broadcasted_iota(jnp.int32, (8, 128), 1)
    line = lax.broadcasted_iota(jnp.int32, (8, 128), 0)
    ends = jnp.where(lane // 64 == line, 1.0, 0.0)

    def one(step, carry):
        start = pl.multiple_of(step * block, block)
        floes = lax.broadcasted_iota(jnp.int32, (block, total), 0) + start
        chosen = hot(floes == index_ref[...])
        both = jnp.dot(chosen, halves[...], preferred_element_type=jnp.float32)
        reply = response_ref[pl.ds(start, block), :]
        product = (both[:, :128] + both[:, 128:]) * jnp.concatenate([reply, reply], axis=1)
        out_ref[:, pl.ds(start, block)] = lax.dot_general(
            ends, product, NT, precision=EXACT, preferred_element_type=jnp.float32
        )
        return carry

    lax.fori_loop(0, out_ref.shape[1] // block, one, 0)


def gather_kernel(index_ref, outline_ref, rim_ref, ox_ref, oy_ref, px_ref, py_ref, table, ox, oy, px, py, sems):
    floes = outline_ref.shape[0]
    inner = pltpu.make_async_copy(outline_ref, table.at[pl.ds(0, floes)], sems.at[0])
    outer = pltpu.make_async_copy(rim_ref, table.at[pl.ds(floes, rim_ref.shape[0])], sems.at[1])
    inner.start()
    outer.start()
    inner.wait()
    outer.wait()
    slots = ox.shape[0]
    half = 2 * TILE

    def one(group, carry):
        for part in range(8):
            slot = group * 8 + part
            own = table[pl.ds(index_ref[0, slot], 1), :]
            own_first = index_ref[1, slot] == 0
            other = table[pl.ds(index_ref[2, slot], 1), :]
            other_first = index_ref[3, slot] == 0
            at = pl.ds(slot, 1)
            ox[at, :] = jnp.where(own_first, own[:, :TILE], own[:, TILE:half])
            oy[at, :] = jnp.where(own_first, own[:, half : half + TILE], own[:, half + TILE :])
            px[at, :] = jnp.where(other_first, other[:, :TILE], other[:, TILE:half])
            py[at, :] = jnp.where(other_first, other[:, half : half + TILE], other[:, half + TILE :])
        return carry

    lax.fori_loop(0, slots // 8, one, 0)
    for source, out in ((ox, ox_ref), (oy, oy_ref), (px, px_ref), (py, py_ref)):
        for start in range(0, slots, 128):
            out[:, start : start + 128] = source[start : start + 128, :].T


def steps_kernel(
    nx, ny, rows, cols, ox_ref, oy_ref, px_ref, py_ref, meta_ref, state_ref, out_ref,
    px2, py2, pq, ax_ref, ay_ref, own_row, own_col, force, state, total, sums,
    first_line, first_side, later_line, later_side, send_sem, recv_sem,
):
    my_x = lax.axis_index("gx")
    my_y = lax.axis_index("gy")
    slots = ox_ref.shape[1]
    high = state_ref.shape[1]

    def present(dx, dy):
        x, y = my_x + dx, my_y + dy
        return (x >= 0) & (x < nx) & (y >= 0) & (y < ny)

    barrier = pltpu.get_barrier_semaphore()
    for dx, dy in zip(DIRX, DIRY):
        @pl.when(present(dx, dy))
        def _():
            pl.semaphore_signal(
                barrier, inc=1, device_id=(my_x + dx, my_y + dy), device_id_type=MESH
            )
    wide = jnp.where(my_x > 0, 2, 1) + jnp.where(my_x < nx - 1, 1, 0)
    deep = jnp.where(my_y > 0, 2, 1) + jnp.where(my_y < ny - 1, 1, 0)
    pl.semaphore_wait(barrier, wide * deep - 1)

    def descriptor(turn, way, source, sign):
        dx, dy = DIRX[way], DIRY[way]
        if dx == 0:
            landing = first_side if turn == 0 else later_side.at[turn - 1]
            landing = landing.at[(dy + 1) // 2]
            part = source
        else:
            landing = first_line if turn == 0 else later_line.at[turn - 1]
            landing = landing.at[way if way < 3 else way - 2]
            part = source.at[:, pl.ds(0 if dx < 0 else rows, 8), :]
        return pltpu.make_async_remote_copy(
            src_ref=part,
            dst_ref=landing,
            send_sem=send_sem.at[turn, way],
            recv_sem=recv_sem.at[turn, way],
            device_id=(my_x + sign * dx, my_y + sign * dy),
            device_id_type=MESH,
        )

    def send(turn, source):
        for way in range(8):
            @pl.when(present(DIRX[way], DIRY[way]))
            def _():
                descriptor(turn, way, source, 1).start()

    def collect(turn, source, into):
        number = into.shape[0]
        for way in range(8):
            dx, dy = DIRX[way], DIRY[way]

            @pl.when(present(-dx, -dy))
            def _():
                descriptor(turn, way, source, -1).wait_recv()
                if dx == 0:
                    landing = first_side if turn == 0 else later_side.at[turn - 1]
                    landing = landing.at[(dy + 1) // 2]
                    top, size = 0, high
                else:
                    landing = first_line if turn == 0 else later_line.at[turn - 1]
                    landing = landing.at[way if way < 3 else way - 2]
                    top, size = (rows if dx < 0 else 0), 8
                lane = lax.broadcasted_iota(jnp.int32, (size, 128), 1)
                line = lax.broadcasted_iota(jnp.int32, (size, 128), 0)
                keep = lane >= 0
                if dx != 0:
                    keep = keep & (line < 2)
                if dy != 0:
                    left = cols if dy < 0 else 0
                    keep = keep & (lane >= left) & (lane < left + 2)
                for part in range(number):
                    piece = landing[part]
                    if dy != 0:
                        piece = pltpu.roll(piece, (cols if dy < 0 else 128 - cols), 1)
                    into[part, top : top + size, :] += jnp.where(keep, piece, 0.0)

    send(0, state_ref)
    state[...] = state_ref[...]

    px = px_ref[...] * SCALE
    py = py_ref[...] * SCALE
    px2[...] = 2.0 * px
    py2[...] = 2.0 * py
    pq[...] = -(px * px + py * py)
    meta = meta_ref[...]
    line_of = jnp.concatenate([meta[0:1], meta[2:3]], axis=1)
    lane_of = jnp.concatenate([meta[1:2], meta[3:4]], axis=1)
    own_row[...] = jnp.where(
        lax.broadcasted_iota(jnp.int32, (high, 2 * slots), 0) == line_of, 1.0, 0.0
    )
    own_col[...] = jnp.where(
        lax.broadcasted_iota(jnp.int32, (128, 2 * slots), 0) == lane_of, 1.0, 0.0
    )
    valid = meta[4:5] > 0
    step_x = meta[5:6].astype(jnp.float32)
    step_y = meta[6:7].astype(jnp.float32)
    collect(0, state_ref, state)
    mass = jnp.where(state[4] == 0.0, 1.0, state[4])

    tall = 64

    for step in range(STEPS):
        shift = jnp.concatenate([state[0], state[1]], axis=0)
        picked = jnp.dot(shift, own_col[...], precision=EXACT, preferred_element_type=jnp.float32)
        at_x = jnp.sum(picked[:high] * own_row[...], axis=0, keepdims=True)
        at_y = jnp.sum(picked[high:] * own_row[...], axis=0, keepdims=True)
        gap_x = at_x[:, :slots] - at_x[:, slots:] - step_x
        gap_y = at_y[:, :slots] - at_y[:, slots:] - step_y
        ax_ref[...] = (ox_ref[...] + gap_x) * SCALE
        ay_ref[...] = (oy_ref[...] + gap_y) * SCALE

        def block(number, carry):
            at = pl.ds(pl.multiple_of(number * 128, 128), 128)
            zero = jnp.zeros((8, 128), jnp.float32)
            along_x, along_y, back_x, back_y = zero, zero, zero, zero
            for start in range(0, TILE, tall):
                ax = ax_ref[start : start + tall, at]
                ay = ay_ref[start : start + tall, at]
                aq = -(ax * ax + ay * ay)

                def vertex(group, sums_now):
                    over_w, bx, by = sums_now
                    base = pl.multiple_of(group * 8, 8)
                    qx = px2[pl.ds(base, 8), at]
                    qy = py2[pl.ds(base, 8), at]
                    qq = pq[pl.ds(base, 8), at]
                    for w in range(8):
                        rx, ry, rq = qx[w : w + 1], qy[w : w + 1], qq[w : w + 1]
                        weight = jnp.exp2((ax * rx + aq) + (ay * ry + rq))
                        over_w = over_w + weight
                        over_u = jnp.sum(weight.reshape(tall // 8, 8, 128), axis=0)
                        bx = bx + over_u * rx
                        by = by + over_u * ry
                    return over_w, bx, by

                over_w, back_x, back_y = lax.fori_loop(
                    0, TILE // 8, vertex,
                    (jnp.zeros((tall, 128), jnp.float32), back_x, back_y),
                )
                along_x = along_x + jnp.sum((ax * over_w).reshape(tall // 8, 8, 128), axis=0)
                along_y = along_y + jnp.sum((ay * over_w).reshape(tall // 8, 8, 128), axis=0)
            force[0:1, at] = jnp.sum(along_x - 0.5 * back_x, axis=0, keepdims=True) / SCALE
            force[1:2, at] = jnp.sum(along_y - 0.5 * back_y, axis=0, keepdims=True) / SCALE
            return carry

        lax.fori_loop(0, slots // 128, block, 0)
        force_x = jnp.where(valid, force[0:1, :], 0.0)
        force_y = jnp.where(valid, force[1:2, :], 0.0)
        both_x = jnp.concatenate([force_x, -force_x], axis=1)
        both_y = jnp.concatenate([force_y, -force_y], axis=1)
        spread = jnp.concatenate([own_row[...] * both_x, own_row[...] * both_y], axis=0)
        placed = lax.dot_general(
            spread, own_col[...], NT, precision=EXACT, preferred_element_type=jnp.float32
        )
        mine = sums.at[step]
        mine[0] = placed[:high]
        mine[1] = placed[high:]
        send(step + 1, mine)
        total[0] = placed[:high]
        total[1] = placed[high:]
        collect(step + 1, mine, total)
        for axis in range(2):
            vel = state[2 + axis]
            vel = vel + DT * ((total[axis] + state[5 + axis]) - DRAG * vel) / mass
            state[2 + axis] = vel
            state[axis] = state[axis] + DT * vel

    out_ref[...] = state[0:4]
    for turn in range(STEPS + 1):
        for way in range(8):
            @pl.when(present(DIRX[way], DIRY[way]))
            def _():
                source = state_ref if turn == 0 else sums.at[turn - 1]
                descriptor(turn, way, source, 1).wait_send()


def table_pick(code, table):
    match = code[:, None] == jnp.arange(8, dtype=jnp.int32)[None, :]
    return jnp.sum(jnp.where(match, jnp.asarray(table, dtype=jnp.int32)[None, :], 0), axis=1)


def neighbours(axis):
    count = lax.axis_size(axis)
    up = [(i, i + 1) for i in range(count - 1)]
    return up, [(j, i) for i, j in up]


def shards(
    outline, centres, velocity, mass, response, pairs, pair_count, forcing, ocean_dest, ocean_floe
):
    rows_x, cols_y, span = outline.shape
    rows_dev, row_width = forcing.shape
    nx, ny = lax.axis_size("gx"), lax.axis_size("gy")
    devices = nx * ny
    floes = rows_x * cols_y
    cap = up_to(max(2, 5 * rows_dev // (2 * devices)), 16)
    params = pltpu.CompilerParams(vmem_limit_bytes=VMEM_BYTES)

    send = pl.pallas_call(
        functools.partial(pack_kernel, devices, cap, cols_y),
        out_shape=jax.ShapeDtypeStruct((devices, cap + 8, row_width), jnp.float32),
        in_specs=[in_vmem()] * 3,
        out_specs=in_vmem(),
        scratch_shapes=[
            pltpu.VMEM((1, rows_dev), jnp.int32),
            pltpu.VMEM((rows_dev, 2 * row_width), jnp.bfloat16),
            pltpu.VMEM((16, rows_dev), jnp.bfloat16),
        ],
        compiler_params=params,
        name="ocean_pack",
    )(ocean_dest.reshape(1, rows_dev), ocean_floe.reshape(1, rows_dev), forcing)
    got = lax.all_to_all(send, ("gx", "gy"), split_axis=0, concat_axis=0, tiled=True)

    up, down = neighbours("gx")
    north = lax.ppermute(outline[rows_x - 1], "gx", up)
    south = lax.ppermute(outline[0], "gx", down)
    up, down = neighbours("gy")
    left = jnp.concatenate([north[None, 0], outline[:, 0], south[None, 0]], axis=0)
    right = jnp.concatenate([north[None, -1], outline[:, -1], south[None, -1]], axis=0)
    west = lax.ppermute(right, "gy", up)
    east = lax.ppermute(left, "gy", down)
    side = up_to(rows_x + 2, 8)
    fill = jnp.zeros((side - rows_x - 2, span), jnp.float32)
    rim = jnp.concatenate([north, south, west, fill, east, fill], axis=0)

    lists = pairs[0, 0]
    slots = lists.shape[0]
    local = jnp.clip(lists[:, 0], 0, floes - 1)
    code = lists[:, 1]
    step_x = table_pick(code, DIRX)
    step_y = table_pick(code, DIRY)
    row = local // cols_y
    col = local % cols_y
    prow = row + step_x
    pcol = col + step_y
    glob_row = lax.axis_index("gx") * rows_x + prow
    glob_col = lax.axis_index("gy") * cols_y + pcol
    inside = (
        (glob_row >= 0) & (glob_row < rows_x * nx) & (glob_col >= 0) & (glob_col < cols_y * ny)
    )
    valid = (jnp.arange(slots, dtype=jnp.int32) < pair_count[0, 0]) & inside
    lines = floes + 2 * cols_y
    other = jnp.where(
        pcol < 0,
        lines + prow + 1,
        jnp.where(
            pcol >= cols_y,
            lines + side + prow + 1,
            jnp.where(
                prow < 0,
                floes + pcol,
                jnp.where(prow >= rows_x, floes + cols_y + pcol, prow * cols_y + pcol),
            ),
        ),
    )
    tiles = jnp.clip(lists[:, 2:], 0, 1)
    index = jnp.stack([local, tiles[:, 0], other, tiles[:, 1]], axis=0)
    nil = jnp.zeros_like(row)
    meta = jnp.stack(
        [row + 1, col + 1, prow + 1, pcol + 1, valid.astype(jnp.int32), step_x, step_y, nil], axis=0
    )
    tile_shape = jax.ShapeDtypeStruct((TILE, slots), jnp.float32)
    tile_sets = pl.pallas_call(
        gather_kernel,
        out_shape=[tile_shape] * 4,
        in_specs=[
            pl.BlockSpec(memory_space=pltpu.SMEM),
            pl.BlockSpec(memory_space=pl.ANY),
            pl.BlockSpec(memory_space=pl.ANY),
        ],
        out_specs=[in_vmem()] * 4,
        scratch_shapes=[pltpu.VMEM((floes + rim.shape[0], span), jnp.float32)]
        + [pltpu.VMEM((slots, TILE), jnp.float32)] * 4
        + [pltpu.SemaphoreType.DMA((2,))],
        compiler_params=params,
        name="gather_tiles",
    )(index, outline.reshape(floes, span), rim)

    names = got[:, cap:, :].reshape(devices, -1)[:, :cap].reshape(1, -1).astype(jnp.int32)
    ocean = pl.pallas_call(
        functools.partial(ocean_kernel, devices, cap),
        out_shape=jax.ShapeDtypeStruct((8, floes), jnp.float32),
        in_specs=[in_vmem()] * 3,
        out_specs=in_vmem(),
        scratch_shapes=[pltpu.VMEM((devices * cap, 2 * row_width), jnp.bfloat16)],
        compiler_params=params,
        name="ocean_force",
    )(names, got, response.reshape(floes, -1))
    ocean = ocean[:2].reshape(2, rows_x, cols_y)

    high = up_to(rows_x + 2, 8)
    state = jnp.concatenate(
        [
            jnp.moveaxis(centres, 2, 0),
            jnp.moveaxis(velocity, 2, 0),
            mass[None],
            ocean,
            jnp.zeros((1, rows_x, cols_y), jnp.float32),
        ],
        axis=0,
    )
    state = jnp.pad(state, ((0, 0), (1, high - rows_x - 1), (1, 128 - cols_y - 1)))
    grid = (high, 128)
    out = pl.pallas_call(
        functools.partial(steps_kernel, nx, ny, rows_x, cols_y),
        out_shape=jax.ShapeDtypeStruct((4,) + grid, jnp.float32),
        in_specs=[in_vmem()] * 6,
        out_specs=in_vmem(),
        scratch_shapes=[pltpu.VMEM((TILE, slots), jnp.float32)] * 5
        + [
            pltpu.VMEM((high, 2 * slots), jnp.float32),
            pltpu.VMEM((128, 2 * slots), jnp.float32),
            pltpu.VMEM((8, slots), jnp.float32),
            pltpu.VMEM((8,) + grid, jnp.float32),
            pltpu.VMEM((2,) + grid, jnp.float32),
            pltpu.VMEM((STEPS, 2) + grid, jnp.float32),
            pltpu.VMEM((6, 8, 8, 128), jnp.float32),
            pltpu.VMEM((2, 8) + grid, jnp.float32),
            pltpu.VMEM((STEPS, 6, 2, 8, 128), jnp.float32),
            pltpu.VMEM((STEPS, 2, 2) + grid, jnp.float32),
            pltpu.SemaphoreType.DMA((STEPS + 1, 8)),
            pltpu.SemaphoreType.DMA((STEPS + 1, 8)),
        ],
        compiler_params=pltpu.CompilerParams(
            vmem_limit_bytes=VMEM_BYTES, collective_id=0, has_side_effects=True
        ),
        name="contact_steps",
    )(*tile_sets, meta, state)
    out = out[:, 1 : rows_x + 1, 1 : cols_y + 1]
    return jnp.moveaxis(out[2:4], 0, 2), jnp.moveaxis(out[0:2], 0, 2)


def solution(mesh):
    return jax.shard_map(
        shards,
        mesh=mesh,
        in_specs=(
            P("gx", "gy", None),
            P("gx", "gy", None),
            P("gx", "gy", None),
            P("gx", "gy"),
            P("gx", "gy", None),
            P("gx", "gy", None, None),
            P("gx", "gy"),
            P(("gx", "gy"), None),
            P(("gx", "gy"), None),
            P(("gx", "gy")),
        ),
        out_specs=(P("gx", "gy", None), P("gx", "gy", None)),
        check_vma=False,
    )
```

```python
import functools
import math

import jax
import jax.numpy as jnp
from jax import lax
from jax.experimental import pallas as pl
from jax.experimental.pallas import tpu as pltpu
from jax.sharding import PartitionSpec as P

MESH = pl.DeviceIdType.MESH
TILE = 128
STEPS = 3

DIRX = (-1, -1, -1, 0, 0, 1, 1, 1)
DIRY = (-1, 0, 1, -1, 1, -1, 0, 1)
INV_WIDTH = 100.0
DT = 0.1
DRAG = 0.5
SCALE = math.sqrt(INV_WIDTH * math.log2(math.e))
NT = (((1,), (1,)), ((), ()))
EXACT = lax.Precision.HIGHEST
VMEM_BYTES = 48 * 1024 * 1024


def up_to(value, step):
    return -(-value // step) * step


def split_two(value):
    high = value.astype(jnp.bfloat16)
    low = (value - high.astype(jnp.float32)).astype(jnp.bfloat16)
    return jnp.concatenate([high, low], axis=1)


def hot(match):
    return jnp.where(match, 1.0, 0.0).astype(jnp.bfloat16)


def in_vmem():
    return pl.BlockSpec(memory_space=pltpu.VMEM)


def pack_kernel(devices, cap, cols, dest_ref, floe_ref, rows_ref, out_ref, place, rank, halves, local):
    count = dest_ref.shape[1]
    width = 256
    before = hot(
        lax.broadcasted_iota(jnp.int32, (width, width), 0)
        < lax.broadcasted_iota(jnp.int32, (width, width), 1)
    )
    owner = lax.broadcasted_iota(jnp.int32, (devices, width), 0)
    offset = jnp.zeros((devices, 1), jnp.float32)
    for start in range(0, count, width):
        dest = dest_ref[:, start : start + width]
        match = owner == dest
        earlier = jnp.dot(hot(match), before, preferred_element_type=jnp.float32) + offset
        slot = jnp.sum(jnp.where(match, earlier, 0.0), axis=0, keepdims=True)
        rank[:, start : start + width] = slot.astype(jnp.int32)
        place[:, start : start + width] = dest * cap + slot.astype(jnp.int32)
        offset = offset + jnp.sum(jnp.where(match, 1.0, 0.0), axis=1, keepdims=True)
    halves[...] = split_two(rows_ref[...])
    floe = floe_ref[...]
    match = lax.broadcasted_iota(jnp.int32, (devices, count), 0) == dest_ref[...]
    named = jnp.concatenate(
        [
            jnp.where(match, (floe // cols).astype(jnp.float32), 0.0),
            jnp.where(match, (floe % cols).astype(jnp.float32), 0.0),
        ],
        axis=0,
    ).astype(jnp.bfloat16)
    ranked = hot(lax.broadcasted_iota(jnp.int32, (cap, count), 0) == rank[...])
    name = lax.dot_general(named, ranked, NT, preferred_element_type=jnp.float32)
    local[...] = name[:devices] * float(cols) + name[devices:]
    group = math.gcd(devices, 4)

    def one(turn, carry):
        first = turn * group
        slots = lax.broadcasted_iota(jnp.int32, (group * cap, count), 0) + first * cap
        chosen = hot(slots == place[...])
        both = jnp.dot(chosen, halves[...], preferred_element_type=jnp.float32)
        both = both[:, :128] + both[:, 128:]
        for part in range(group):
            device = first + part
            out_ref[device, 0:cap, :] = both[part * cap : (part + 1) * cap]
            out_ref[device, cap : cap + 8, :] = jnp.zeros((8, 128), jnp.float32)
            mine = local[pl.ds(device, 1), :]
            for start in range(0, cap, 128):
                size = min(128, cap - start)
                line = cap + start // 128
                out_ref[device, line : line + 1, 0:size] = mine[:, start : start + size]
        return carry

    lax.fori_loop(0, devices // group, one, 0)


def ocean_kernel(devices, cap, index_ref, rows_ref, response_ref, out_ref, halves):
    total = devices * cap
    block = 256

    def split(device, carry):
        start = pl.multiple_of(device * cap, 16)
        halves[pl.ds(start, cap), :] = split_two(rows_ref[device, 0:cap, :])
        return carry

    lax.fori_loop(0, devices, split, 0)
    lane = lax.broadcasted_iota(jnp.int32, (8, 128), 1)
    line = lax.broadcasted_iota(jnp.int32, (8, 128), 0)
    ends = jnp.where(lane // 64 == line, 1.0, 0.0)

    def one(step, carry):
        start = pl.multiple_of(step * block, block)
        floes = lax.broadcasted_iota(jnp.int32, (block, total), 0) + start
        chosen = hot(floes == index_ref[...])
        both = jnp.dot(chosen, halves[...], preferred_element_type=jnp.float32)
        reply = response_ref[pl.ds(start, block), :]
        product = (both[:, :128] + both[:, 128:]) * jnp.concatenate([reply, reply], axis=1)
        out_ref[:, pl.ds(start, block)] = lax.dot_general(
            ends, product, NT, precision=EXACT, preferred_element_type=jnp.float32
        )
        return carry

    lax.fori_loop(0, out_ref.shape[1] // block, one, 0)


def gather_kernel(index_ref, outline_ref, rim_ref, ox_ref, oy_ref, px_ref, py_ref, table, ox, oy, px, py, sems):
    floes = outline_ref.shape[0]
    inner = pltpu.make_async_copy(outline_ref, table.at[pl.ds(0, floes)], sems.at[0])
    outer = pltpu.make_async_copy(rim_ref, table.at[pl.ds(floes, rim_ref.shape[0])], sems.at[1])
    inner.start()
    outer.start()
    inner.wait()
    outer.wait()
    slots = ox.shape[0]
    half = 2 * TILE

    def one(group, carry):
        for part in range(8):
            slot = group * 8 + part
            own = table[pl.ds(index_ref[0, slot], 1), :]
            own_first = index_ref[1, slot] == 0
            other = table[pl.ds(index_ref[2, slot], 1), :]
            other_first = index_ref[3, slot] == 0
            at = pl.ds(slot, 1)
            ox[at, :] = jnp.where(own_first, own[:, :TILE], own[:, TILE:half])
            oy[at, :] = jnp.where(own_first, own[:, half : half + TILE], own[:, half + TILE :])
            px[at, :] = jnp.where(other_first, other[:, :TILE], other[:, TILE:half])
            py[at, :] = jnp.where(other_first, other[:, half : half + TILE], other[:, half + TILE :])
        return carry

    lax.fori_loop(0, slots // 8, one, 0)
    for source, out in ((ox, ox_ref), (oy, oy_ref), (px, px_ref), (py, py_ref)):
        for start in range(0, slots, 128):
            out[:, start : start + 128] = source[start : start + 128, :].T


def steps_kernel(nx, ny, rows, cols, opening, ox_ref, oy_ref, px_ref, py_ref, meta_ref, state_ref, *refs):
    if opening:
        state_out, total_out = refs[:2]
        refs = refs[2:]
        first_sent = state_ref
    else:
        wave_ref, contact_ref, out_ref = refs[:3]
        refs = refs[3:]
        first_sent = wave_ref
    (
        px2, py2, pq, ax_ref, ay_ref, own_row, own_col, force, state, wave, total, sums,
        first_line, first_side, later_line, later_side, send_sem, recv_sem,
    ) = refs
    steps = 1 if opening else STEPS - 1
    my_x = lax.axis_index("gx")
    my_y = lax.axis_index("gy")
    slots = ox_ref.shape[1]
    high = state_ref.shape[1]

    def present(dx, dy):
        x, y = my_x + dx, my_y + dy
        return (x >= 0) & (x < nx) & (y >= 0) & (y < ny)

    barrier = pltpu.get_barrier_semaphore()
    for dx, dy in zip(DIRX, DIRY):
        @pl.when(present(dx, dy))
        def _():
            pl.semaphore_signal(
                barrier, inc=1, device_id=(my_x + dx, my_y + dy), device_id_type=MESH
            )
    wide = jnp.where(my_x > 0, 2, 1) + jnp.where(my_x < nx - 1, 1, 0)
    deep = jnp.where(my_y > 0, 2, 1) + jnp.where(my_y < ny - 1, 1, 0)
    pl.semaphore_wait(barrier, wide * deep - 1)

    def descriptor(turn, way, source, sign):
        dx, dy = DIRX[way], DIRY[way]
        if dx == 0:
            landing = first_side if turn == 0 else later_side.at[turn - 1]
            landing = landing.at[(dy + 1) // 2]
            part = source
        else:
            landing = first_line if turn == 0 else later_line.at[turn - 1]
            landing = landing.at[way if way < 3 else way - 2]
            part = source.at[:, pl.ds(0 if dx < 0 else rows, 8), :]
        return pltpu.make_async_remote_copy(
            src_ref=part,
            dst_ref=landing,
            send_sem=send_sem.at[turn, way],
            recv_sem=recv_sem.at[turn, way],
            device_id=(my_x + sign * dx, my_y + sign * dy),
            device_id_type=MESH,
        )

    def send(turn, source):
        for way in range(8):
            @pl.when(present(DIRX[way], DIRY[way]))
            def _():
                descriptor(turn, way, source, 1).start()

    def collect(turn, source, into):
        number = into.shape[0]
        for way in range(8):
            dx, dy = DIRX[way], DIRY[way]

            @pl.when(present(-dx, -dy))
            def _():
                descriptor(turn, way, source, -1).wait_recv()
                if dx == 0:
                    landing = first_side if turn == 0 else later_side.at[turn - 1]
                    landing = landing.at[(dy + 1) // 2]
                    top, size = 0, high
                else:
                    landing = first_line if turn == 0 else later_line.at[turn - 1]
                    landing = landing.at[way if way < 3 else way - 2]
                    top, size = (rows if dx < 0 else 0), 8
                lane = lax.broadcasted_iota(jnp.int32, (size, 128), 1)
                line = lax.broadcasted_iota(jnp.int32, (size, 128), 0)
                keep = lane >= 0
                if dx != 0:
                    keep = keep & (line < 2)
                if dy != 0:
                    left = cols if dy < 0 else 0
                    keep = keep & (lane >= left) & (lane < left + 2)
                for part in range(number):
                    piece = landing[part]
                    if dy != 0:
                        piece = pltpu.roll(piece, (cols if dy < 0 else 128 - cols), 1)
                    into[part, top : top + size, :] += jnp.where(keep, piece, 0.0)

    send(0, first_sent)
    state[...] = state_ref[...]
    if not opening:
        wave[...] = wave_ref[...]

    px = px_ref[...] * SCALE
    py = py_ref[...] * SCALE
    px2[...] = 2.0 * px
    py2[...] = 2.0 * py
    pq[...] = -(px * px + py * py)
    meta = meta_ref[...]
    line_of = jnp.concatenate([meta[0:1], meta[2:3]], axis=1)
    lane_of = jnp.concatenate([meta[1:2], meta[3:4]], axis=1)
    own_row[...] = jnp.where(
        lax.broadcasted_iota(jnp.int32, (high, 2 * slots), 0) == line_of, 1.0, 0.0
    )
    own_col[...] = jnp.where(
        lax.broadcasted_iota(jnp.int32, (128, 2 * slots), 0) == lane_of, 1.0, 0.0
    )
    valid = meta[4:5] > 0
    step_x = meta[5:6].astype(jnp.float32)
    step_y = meta[6:7].astype(jnp.float32)

    def advance(contact):
        mass = jnp.where(state[4] == 0.0, 1.0, state[4])
        for axis in range(2):
            vel = state[2 + axis]
            vel = vel + DT * ((contact[axis] + wave[axis]) - DRAG * vel) / mass
            state[2 + axis] = vel
            state[axis] = state[axis] + DT * vel

    if opening:
        collect(0, state_ref, state)
        state_out[...] = state[...]
    else:
        collect(0, wave_ref, wave)
        advance(contact_ref)

    tall = 64

    for step in range(steps):
        shift = jnp.concatenate([state[0], state[1]], axis=0)
        picked = jnp.dot(shift, own_col[...], precision=EXACT, preferred_element_type=jnp.float32)
        at_x = jnp.sum(picked[:high] * own_row[...], axis=0, keepdims=True)
        at_y = jnp.sum(picked[high:] * own_row[...], axis=0, keepdims=True)
        gap_x = at_x[:, :slots] - at_x[:, slots:] - step_x
        gap_y = at_y[:, :slots] - at_y[:, slots:] - step_y
        ax_ref[...] = (ox_ref[...] + gap_x) * SCALE
        ay_ref[...] = (oy_ref[...] + gap_y) * SCALE

        def block(number, carry):
            at = pl.ds(pl.multiple_of(number * 128, 128), 128)
            zero = jnp.zeros((8, 128), jnp.float32)
            along_x, along_y, back_x, back_y = zero, zero, zero, zero
            for start in range(0, TILE, tall):
                ax = ax_ref[start : start + tall, at]
                ay = ay_ref[start : start + tall, at]
                aq = -(ax * ax + ay * ay)

                def vertex(group, sums_now):
                    over_w, bx, by = sums_now
                    base = pl.multiple_of(group * 8, 8)
                    qx = px2[pl.ds(base, 8), at]
                    qy = py2[pl.ds(base, 8), at]
                    qq = pq[pl.ds(base, 8), at]
                    for w in range(8):
                        rx, ry, rq = qx[w : w + 1], qy[w : w + 1], qq[w : w + 1]
                        weight = jnp.exp2((ax * rx + aq) + (ay * ry + rq))
                        over_w = over_w + weight
                        over_u = jnp.sum(weight.reshape(tall // 8, 8, 128), axis=0)
                        bx = bx + over_u * rx
                        by = by + over_u * ry
                    return over_w, bx, by

                over_w, back_x, back_y = lax.fori_loop(
                    0, TILE // 8, vertex,
                    (jnp.zeros((tall, 128), jnp.float32), back_x, back_y),
                )
                along_x = along_x + jnp.sum((ax * over_w).reshape(tall // 8, 8, 128), axis=0)
                along_y = along_y + jnp.sum((ay * over_w).reshape(tall // 8, 8, 128), axis=0)
            force[0:1, at] = jnp.sum(along_x - 0.5 * back_x, axis=0, keepdims=True) / SCALE
            force[1:2, at] = jnp.sum(along_y - 0.5 * back_y, axis=0, keepdims=True) / SCALE
            return carry

        lax.fori_loop(0, slots // 128, block, 0)
        force_x = jnp.where(valid, force[0:1, :], 0.0)
        force_y = jnp.where(valid, force[1:2, :], 0.0)
        both_x = jnp.concatenate([force_x, -force_x], axis=1)
        both_y = jnp.concatenate([force_y, -force_y], axis=1)
        spread = jnp.concatenate([own_row[...] * both_x, own_row[...] * both_y], axis=0)
        placed = lax.dot_general(
            spread, own_col[...], NT, precision=EXACT, preferred_element_type=jnp.float32
        )
        mine = sums.at[step]
        mine[0] = placed[:high]
        mine[1] = placed[high:]
        send(step + 1, mine)
        total[0] = placed[:high]
        total[1] = placed[high:]
        collect(step + 1, mine, total)
        if not opening:
            advance(total)

    if opening:
        total_out[...] = total[...]
    else:
        out_ref[...] = state[0:4]
    for turn in range(steps + 1):
        for way in range(8):
            @pl.when(present(DIRX[way], DIRY[way]))
            def _():
                source = first_sent if turn == 0 else sums.at[turn - 1]
                descriptor(turn, way, source, 1).wait_send()


def table_pick(code, table):
    match = code[:, None] == jnp.arange(8, dtype=jnp.int32)[None, :]
    return jnp.sum(jnp.where(match, jnp.asarray(table, dtype=jnp.int32)[None, :], 0), axis=1)


def neighbours(axis):
    count = lax.axis_size(axis)
    up = [(i, i + 1) for i in range(count - 1)]
    return up, [(j, i) for i, j in up]


def shards(
    outline, centres, velocity, mass, response, pairs, pair_count, forcing, ocean_dest, ocean_floe
):
    rows_x, cols_y, span = outline.shape
    rows_dev, row_width = forcing.shape
    nx, ny = lax.axis_size("gx"), lax.axis_size("gy")
    devices = nx * ny
    floes = rows_x * cols_y
    cap = up_to(max(2, 5 * rows_dev // (2 * devices)), 16)
    params = pltpu.CompilerParams(vmem_limit_bytes=VMEM_BYTES)

    send = pl.pallas_call(
        functools.partial(pack_kernel, devices, cap, cols_y),
        out_shape=jax.ShapeDtypeStruct((devices, cap + 8, row_width), jnp.float32),
        in_specs=[in_vmem()] * 3,
        out_specs=in_vmem(),
        scratch_shapes=[
            pltpu.VMEM((1, rows_dev), jnp.int32),
            pltpu.VMEM((1, rows_dev), jnp.int32),
            pltpu.VMEM((rows_dev, 2 * row_width), jnp.bfloat16),
            pltpu.VMEM((devices, cap), jnp.float32),
        ],
        cost_estimate=pl.CostEstimate(
            flops=4 * devices * cap * rows_dev * row_width, bytes_accessed=10**7, transcendentals=0
        ),
        compiler_params=params,
        name="ocean_pack",
    )(ocean_dest.reshape(1, rows_dev), ocean_floe.reshape(1, rows_dev), forcing)
    up, down = neighbours("gx")
    north = lax.ppermute(outline[rows_x - 1], "gx", up)
    south = lax.ppermute(outline[0], "gx", down)
    up, down = neighbours("gy")
    left = jnp.concatenate([north[None, 0], outline[:, 0], south[None, 0]], axis=0)
    right = jnp.concatenate([north[None, -1], outline[:, -1], south[None, -1]], axis=0)
    west = lax.ppermute(right, "gy", up)
    east = lax.ppermute(left, "gy", down)
    side = up_to(rows_x + 2, 8)
    fill = jnp.zeros((side - rows_x - 2, span), jnp.float32)
    rim = jnp.concatenate([north, south, west, fill, east, fill], axis=0)
    rim, send = lax.optimization_barrier((rim, send))
    got = lax.all_to_all(send, ("gx", "gy"), split_axis=0, concat_axis=0, tiled=True)

    lists = pairs[0, 0]
    slots = lists.shape[0]
    local = jnp.clip(lists[:, 0], 0, floes - 1)
    code = lists[:, 1]
    step_x = table_pick(code, DIRX)
    step_y = table_pick(code, DIRY)
    row = local // cols_y
    col = local % cols_y
    prow = row + step_x
    pcol = col + step_y
    glob_row = lax.axis_index("gx") * rows_x + prow
    glob_col = lax.axis_index("gy") * cols_y + pcol
    inside = (
        (glob_row >= 0) & (glob_row < rows_x * nx) & (glob_col >= 0) & (glob_col < cols_y * ny)
    )
    valid = (jnp.arange(slots, dtype=jnp.int32) < pair_count[0, 0]) & inside
    lines = floes + 2 * cols_y
    other = jnp.where(
        pcol < 0,
        lines + prow + 1,
        jnp.where(
            pcol >= cols_y,
            lines + side + prow + 1,
            jnp.where(
                prow < 0,
                floes + pcol,
                jnp.where(prow >= rows_x, floes + cols_y + pcol, prow * cols_y + pcol),
            ),
        ),
    )
    tiles = jnp.clip(lists[:, 2:], 0, 1)
    index = jnp.stack([local, tiles[:, 0], other, tiles[:, 1]], axis=0)
    nil = jnp.zeros_like(row)
    meta = jnp.stack(
        [row + 1, col + 1, prow + 1, pcol + 1, valid.astype(jnp.int32), step_x, step_y, nil], axis=0
    )
    tile_shape = jax.ShapeDtypeStruct((TILE, slots), jnp.float32)
    tile_sets = pl.pallas_call(
        gather_kernel,
        out_shape=[tile_shape] * 4,
        in_specs=[
            pl.BlockSpec(memory_space=pltpu.SMEM),
            pl.BlockSpec(memory_space=pl.ANY),
            pl.BlockSpec(memory_space=pl.ANY),
        ],
        out_specs=[in_vmem()] * 4,
        scratch_shapes=[pltpu.VMEM((floes + rim.shape[0], span), jnp.float32)]
        + [pltpu.VMEM((slots, TILE), jnp.float32)] * 4
        + [pltpu.SemaphoreType.DMA((2,))],
        compiler_params=params,
        name="gather_tiles",
    )(index, outline.reshape(floes, span), rim)

    high = up_to(rows_x + 2, 8)
    grid = (high, 128)

    def rimmed(parts):
        return jnp.pad(parts, ((0, 0), (1, high - rows_x - 1), (1, 128 - cols_y - 1)))

    def contact_call(opening, out_shape, *operands):
        steps = 1 if opening else STEPS - 1
        sent = 8 if opening else 2
        return pl.pallas_call(
            functools.partial(steps_kernel, nx, ny, rows_x, cols_y, opening),
            out_shape=out_shape,
            in_specs=[in_vmem()] * len(operands),
            out_specs=jax.tree.map(lambda _: in_vmem(), out_shape),
            scratch_shapes=[pltpu.VMEM((TILE, slots), jnp.float32)] * 5
            + [
                pltpu.VMEM((high, 2 * slots), jnp.float32),
                pltpu.VMEM((128, 2 * slots), jnp.float32),
                pltpu.VMEM((8, slots), jnp.float32),
                pltpu.VMEM((8,) + grid, jnp.float32),
                pltpu.VMEM((2,) + grid, jnp.float32),
                pltpu.VMEM((2,) + grid, jnp.float32),
                pltpu.VMEM((steps, 2) + grid, jnp.float32),
                pltpu.VMEM((6, sent, 8, 128), jnp.float32),
                pltpu.VMEM((2, sent) + grid, jnp.float32),
                pltpu.VMEM((steps, 6, 2, 8, 128), jnp.float32),
                pltpu.VMEM((steps, 2, 2) + grid, jnp.float32),
                pltpu.SemaphoreType.DMA((steps + 1, 8)),
                pltpu.SemaphoreType.DMA((steps + 1, 8)),
            ],
            cost_estimate=pl.CostEstimate(
                flops=steps * 10 * slots * TILE * TILE,
                bytes_accessed=10**8,
                transcendentals=steps * slots * TILE * TILE,
            ),
            compiler_params=pltpu.CompilerParams(
                vmem_limit_bytes=VMEM_BYTES,
                collective_id=0 if opening else 1,
                has_side_effects=True,
            ),
            name="contact_opening" if opening else "contact_steps",
        )(*operands)

    state = rimmed(
        jnp.concatenate(
            [
                jnp.moveaxis(centres, 2, 0),
                jnp.moveaxis(velocity, 2, 0),
                mass[None],
                jnp.zeros((3, rows_x, cols_y), jnp.float32),
            ],
            axis=0,
        )
    )
    state, contact = contact_call(
        True,
        [jax.ShapeDtypeStruct((n,) + grid, jnp.float32) for n in (8, 2)],
        *tile_sets, meta, state,
    )

    response, contact = lax.optimization_barrier((response, contact))
    names = got[:, cap:, :].reshape(devices, -1)[:, :cap].reshape(1, -1).astype(jnp.int32)
    ocean = pl.pallas_call(
        functools.partial(ocean_kernel, devices, cap),
        out_shape=jax.ShapeDtypeStruct((8, floes), jnp.float32),
        in_specs=[in_vmem()] * 3,
        out_specs=in_vmem(),
        scratch_shapes=[pltpu.VMEM((devices * cap, 2 * row_width), jnp.bfloat16)],
        compiler_params=params,
        name="ocean_force",
    )(names, got, response.reshape(floes, -1))
    ocean = ocean[:2].reshape(2, rows_x, cols_y)

    out = contact_call(
        False,
        jax.ShapeDtypeStruct((4,) + grid, jnp.float32),
        *tile_sets, meta, state, rimmed(ocean), contact,
    )
    out = out[:, 1 : rows_x + 1, 1 : cols_y + 1]
    return jnp.moveaxis(out[2:4], 0, 2), jnp.moveaxis(out[0:2], 0, 2)


def solution(mesh):
    return jax.shard_map(
        shards,
        mesh=mesh,
        in_specs=(
            P("gx", "gy", None),
            P("gx", "gy", None),
            P("gx", "gy", None),
            P("gx", "gy"),
            P("gx", "gy", None),
            P("gx", "gy", None, None),
            P("gx", "gy"),
            P(("gx", "gy"), None),
            P(("gx", "gy"), None),
            P(("gx", "gy")),
        ),
        out_specs=(P("gx", "gy", None), P("gx", "gy", None)),
        check_vma=False,
    )
```
